512 devices in a mesh: rep: 16 (over y_hi, x), section: 32 (over y_lo, z, core).
Axes of the slice: x: 4, y: 8 (y_hi: 4, y_lo: 2; y = y_hi * 2 + y_lo), z: 8, core: 2. Of those that a mesh axis runs over, the one named last changes fastest.
Arguments:
- features: bfloat16 [65536, 128], P(('rep', 'section')), may hold values from -6 to 6
- adj_tiles: bfloat16 [65536, 128, 128], P(('rep', 'section')), may hold values from -0.0625 to 0.0625
- tile_rows: int32 [65536], P(('rep', 'section')), may hold values from 0 to 15
- tile_cols: int32 [65536], P(('rep', 'section')), may hold values from 0 to 31
- tile_counts: int32 [512], P(('rep', 'section')), may hold values from 32 to 128, as said below
- weight: bfloat16 [128, 256], replicated, may hold values from -0.5 to 0.5
- out_bias: float32 [256], replicated, may hold values from -3 to 3
Outputs:
- hidden_out: bfloat16 [65536, 256], P(('rep', 'section'))
The draws below stay inside these ranges and needn't reach their ends.
Inputs may be any that keep to these rules, and one draw needn't show every extreme that they name: `tile_counts`: slots of a device at or beyond its count hold no tile; some device uses all 128 slots in every draw.
All inputs are finite; a program needn't handle non-finite values.
Results may differ from the reference program's by a relative error of at most 0.02.
Values may be sent and summed in bfloat16 or wider, within the bound.
A program may use at most 64 MiB of HBM per device.

```python
import jax
import jax.numpy as jnp
from jax import lax

F = 128
H = 256
TILE = 128
BLK_DEV = 1
TILES_DEV = 128
NODES = 65536
ROW_BLOCKS = 16
COL_BLOCKS = 32
SLOTS = 65536
N_REP = 16
N_SECTION = 32


def draw_tile_counts(key, part):
    key = jax.random.fold_in(key, 7)
    key_pick, key_heavy, key_base = jax.random.split(key, 3)
    chosen = jax.random.randint(key_pick, (), 0, N_REP * N_SECTION)
    heavy = jax.random.randint(key_heavy, (N_REP * N_SECTION,), 0, 16) == 0
    heavy = heavy | (jnp.arange(N_REP * N_SECTION) == chosen)
    light = TILES_DEV // 4 + jax.random.randint(key_base, (N_REP * N_SECTION,), 0, TILES_DEV // 4 + 1)
    return jnp.where(heavy, TILES_DEV, light).astype(jnp.int32)


def set_ends(drawn, stream_key, smallest, largest):
    dims = drawn.shape
    place = [jax.random.randint(jax.random.fold_in(stream_key, axis), (), 0, dims[axis]) for axis in range(len(dims))]
    drawn = drawn.at[tuple(place)].set(smallest)
    longest = dims.index(max(dims))
    place[longest] = (place[longest] + 1) % dims[longest]
    return drawn.at[tuple(place)].set(largest)


def block_scale(stream_key, dims, pieces, least, top_value):
    level, own = 1.0, jax.random.fold_in(stream_key, 6)
    for dim, shards_of in pieces:
        heights = jnp.exp(jax.random.uniform(jax.random.fold_in(own, dim), (shards_of,), jnp.float32, least / len(pieces), top_value / len(pieces)))
        level = level * jnp.repeat(heights, dims[dim] // shards_of).reshape([-1 if axis == dim else 1 for axis in range(len(dims))])
    return level


def scatter_about(own_key, dims, scale, bound, cuts=(), kind=jnp.bfloat16):
    array = scale * jax.random.normal(own_key, dims, jnp.float32)
    if cuts:
        array = array * block_scale(own_key, dims, cuts, -0.22, 0.18)
    return jnp.clip(array, -bound, bound).astype(kind)


def setup_inputs(seed: int = 0) -> dict:
    keys = jax.random.split(jax.random.key(seed), 8)
    features = scatter_about(keys[0], (NODES, F), 1.0, 6.0, ((0, 512),))
    adj_tiles = scatter_about(keys[1], (SLOTS, TILE, TILE), (TILE * TILES_DEV // 2) ** -0.5, 0.0625, ((0, 512),))
    tile_rows = set_ends(jax.random.randint(keys[2], (SLOTS,), 0, ROW_BLOCKS), jax.random.fold_in(keys[2], 1), 0, ROW_BLOCKS - 1).astype(jnp.int32)
    tile_cols = set_ends(jax.random.randint(keys[3], (SLOTS,), 0, COL_BLOCKS), jax.random.fold_in(keys[3], 1), 0, COL_BLOCKS - 1).astype(jnp.int32)
    tile_counts = draw_tile_counts(jax.random.fold_in(keys[7], 71), 0)
    weight = scatter_about(keys[5], (F, H), F ** -0.5, 0.5)
    out_bias = scatter_about(keys[6], (H,), 0.5, 3.0, (), jnp.float32)
    return dict(features=features, adj_tiles=adj_tiles, tile_rows=tile_rows, tile_cols=tile_cols, tile_counts=tile_counts, weight=weight, out_bias=out_bias)


def reference(features, adj_tiles, tile_rows, tile_cols, tile_counts, weight, out_bias):
    feat_groups = features.reshape(N_REP, COL_BLOCKS, TILE, F)
    tile_groups = adj_tiles.reshape(N_REP, N_SECTION, TILES_DEV, TILE, TILE)
    row_index = tile_rows.reshape(N_REP, N_SECTION, TILES_DEV)
    col_index = tile_cols.reshape(N_REP, N_SECTION, TILES_DEV)
    used = tile_counts.reshape(N_REP, N_SECTION)

    def section_sum(section_id):
        def rep_step(carry, rep_id):
            group = feat_groups[rep_id]
            sources = jnp.take(group, col_index[rep_id, section_id], axis=0)
            products = jnp.einsum('tij,tjk->tik', tile_groups[rep_id, section_id].astype(jnp.float32), sources.astype(jnp.float32), precision=lax.Precision.HIGHEST)
            live_slots = jnp.arange(TILES_DEV) < used[rep_id, section_id]
            products = jnp.where(live_slots[:, None, None], products, jnp.float32(0.0))
            partial_value = jax.ops.segment_sum(products, row_index[rep_id, section_id], num_segments=ROW_BLOCKS)
            partial_value = partial_value.astype(jnp.bfloat16).reshape(ROW_BLOCKS * TILE, F)
            return carry + jnp.dot(partial_value, weight, preferred_element_type=jnp.float32), None

        start = jnp.zeros((ROW_BLOCKS * TILE, H), jnp.float32)
        summed, unused = lax.scan(rep_step, start, jnp.arange(N_REP))
        return summed

    sums = lax.map(section_sum, jnp.arange(N_SECTION))
    sums = sums.reshape(N_SECTION, N_REP, BLK_DEV * TILE, H).transpose(1, 0, 2, 3).reshape(NODES, H)
    return jax.nn.relu(sums + out_bias).astype(jnp.bfloat16)
```

```python
import jax
import jax.numpy as jnp
from jax import lax
from jax.experimental import pallas as pl
from jax.experimental.pallas import tpu as pltpu
from jax.sharding import PartitionSpec as P

MESH = pl.DeviceIdType.MESH
NX, NY, NZ = 4, 4, 8
RELAYS = NZ // 2 - 1

HALF = 64


def kernel(
    features, adjacency, rows_in, cols_in, count_in, weight_in, bias_in, out_ref,
    rows_ref, cols_ref, count_ref, weight, bias,
    slab, tiles, sums, plan_v, plan, outbox, inbox_x, relay_y, inbox_y,
    local_sem, send_z, recv_z, send_y, recv_y, send_c, recv_c, send_px, recv_px, send_py, recv_py,
):
    rep, section = lax.axis_index("rep"), lax.axis_index("section")
    yh, x = rep // NX, rep % NX
    y, z, core = section // (2 * NZ), (section // 2) % NZ, section % 2
    z_up = y * 2 * NZ + ((z + 1) % NZ) * 2 + core
    z_down = y * 2 * NZ + ((z + NZ - 1) % NZ) * 2 + core
    partner = (1 - y) * 2 * NZ + z * 2 + core
    sibling = section + 1 - 2 * core

    def x_peer(step):
        return yh * NX + (x + step) % NX

    def y_peer(step):
        return ((yh + step) % NY) * NX + x

    def base(at):
        return (at * 2 + core) * 4

    own_rows = slab.at[pl.ds(base(z) + 1, 2)]
    small = [
        pltpu.make_async_copy(source, target, local_sem.at[3 + i])
        for i, (source, target) in enumerate(
            ((rows_in, rows_ref), (cols_in, cols_ref), (count_in, count_ref), (weight_in, weight), (bias_in, bias))
        )
    ]
    tile_copy = pltpu.make_async_copy(adjacency, tiles, local_sem.at[0])
    own_copy = pltpu.make_async_copy(features, own_rows, local_sem.at[1])
    own_copy.start()
    for copy in small:
        copy.start()
    tile_copy.start()

    barrier = pltpu.get_barrier_semaphore()
    for peer in (z_up, z_down, partner, sibling):
        pl.semaphore_signal(barrier, inc=1, device_id={"section": peer}, device_id_type=MESH)
    for step in range(1, NX):
        pl.semaphore_signal(barrier, inc=1, device_id={"rep": x_peer(step)}, device_id_type=MESH)
    for step in range(1, NY):
        pl.semaphore_signal(barrier, inc=1, device_id={"rep": y_peer(step)}, device_id_type=MESH)
    own_copy.wait()
    pl.semaphore_wait(barrier, 4 + NX - 1 + NY - 1)

    sent = []

    def piece(at, begin, count):
        return slab.at[pl.ds(base(at) + begin, count)]

    def push(source, target, send, recv, peer):
        copy = pltpu.make_async_remote_copy(
            src_ref=source, dst_ref=target, send_sem=send, recv_sem=recv,
            device_id=peer, device_id_type=MESH,
        )
        copy.start()
        sent.append(copy)
        return copy

    def along_z(way, step, kind):
        at = (z - step + NZ) % NZ if way == 0 else (z + step) % NZ
        last = step == RELAYS
        if kind == 0:
            ref = piece(at, 1 + way, 1) if last else piece(at, 1, 2)
        elif last:
            ref = slab.at[base(at), pl.ds(way * (HALF // 2), HALF // 2)]
        else:
            ref = piece(at, 0, 1)
        return push(ref, ref, send_z.at[way, step, kind], recv_z.at[way, step, kind], {"section": (z_up, z_down)[way]})

    def to_partner(at, slot, begin, target):
        return push(piece(at, begin, 1), piece(at, target, 1), send_y.at[slot], recv_y.at[slot], {"section": partner})

    def to_sibling(at, slot, part):
        ref = piece(at, *((1, 2), (0, 1), (3, 1))[part])
        return push(ref, ref, send_c.at[slot, part], recv_c.at[slot, part], {"section": sibling})

    def origin(way, step):
        return (z - step - 1 + NZ) % NZ if way == 0 else (z + step + 1) % NZ

    def slot_of(way, step):
        return 1 + 2 * step + way

    first = to_partner(z, NZ, 1, 0)
    wide = [along_z(0, 0, 0), along_z(1, 0, 0)]
    lower = [(z, 0, to_partner(z, 0, 2, 3))]
    siblings = [to_sibling(z, 0, 0)]

    for copy in small:
        copy.wait()
    lane = lax.broadcasted_iota(jnp.int32, (128, 128), 1)
    down = lax.broadcasted_iota(jnp.int32, (128, 128), 0)
    row_across = jnp.broadcast_to(rows_ref[...], (128, 128))
    row_across = jnp.where(lane < jnp.broadcast_to(count_ref[...], (128, 128)), row_across, NX * NY)
    key_across = row_across * 128 + lane
    key_down = key_across.T
    rank = jnp.sum((key_down < key_across).astype(jnp.int32), axis=0, keepdims=True)
    rank_down = jnp.broadcast_to(rank, (128, 128)).T
    col_across = jnp.broadcast_to(cols_ref[...], (128, 128))
    info_across = lane + col_across * 128 + row_across * 4096
    info_down = info_across.T
    row_down = key_down // 128
    order = jnp.sum(jnp.where(rank_down == lane, info_down, 0), axis=0, keepdims=True)
    ends = jnp.sum((row_down <= lane).astype(jnp.int32), axis=0, keepdims=True)
    used = jnp.sum((row_down == lane).astype(jnp.int32), axis=0, keepdims=True)
    line = lax.broadcasted_iota(jnp.int32, (8, 128), 0)
    plan_v[...] = jnp.where(line == 0, order, jnp.where(line == 1, ends, used))
    plan_copy = pltpu.make_async_copy(plan_v, plan, local_sem.at[2])
    plan_copy.start()

    first.wait_recv()
    narrow = [along_z(0, 0, 1), along_z(1, 0, 1)]
    siblings.append(to_sibling(z, 0, 1))
    for step in range(RELAYS):
        arrived, wide_next, narrow_next = lower, [], []
        lower = []
        for way in range(2):
            wide[way].wait_recv()
            wide_next.append(along_z(way, step + 1, 0))
            at, slot = origin(way, step), slot_of(way, step)
            lower.append((at, slot, to_partner(at, slot, 2, 3)))
            siblings.append(to_sibling(at, slot, 0))
        for way in range(2):
            narrow[way].wait_recv()
            narrow_next.append(along_z(way, step + 1, 1))
            siblings.append(to_sibling(origin(way, step), slot_of(way, step), 1))
        for at, slot, copy in arrived:
            copy.wait_recv()
            siblings.append(to_sibling(at, slot, 2))
        wide, narrow = wide_next, narrow_next
    far = (z + NZ // 2) % NZ
    far_slot = NZ - 1
    wide[1].wait_recv()
    lower.append((far, far_slot, to_partner(far, far_slot, 2, 3)))
    wide[0].wait_recv()
    siblings.append(to_sibling(far, far_slot, 0))
    for way in range(2):
        narrow[way].wait_recv()
    siblings.append(to_sibling(far, far_slot, 1))
    for at, slot, copy in lower:
        copy.wait_recv()
        siblings.append(to_sibling(at, slot, 2))
    plan_copy.wait()
    tile_copy.wait()
    for copy in siblings:
        copy.wait_recv()

    def step_of(k, carry):
        total, row_before = carry
        info = plan[0, k]
        slot, col, row = info & 127, (info >> 7) & 31, info >> 12
        other = (col >> 4) ^ y
        at = (col & 15) * 4
        source = jnp.concatenate([slab[at + 1 - other], slab[at + 2 + other]], axis=0)
        product = jnp.dot(tiles[slot], source, preferred_element_type=jnp.float32)
        total = total * jnp.where(row == row_before, 1.0, 0.0) + product
        sums[k] = total
        return total, row

    lax.fori_loop(0, 128, step_of, (jnp.zeros((128, 128), jnp.float32), jnp.int32(-1)), unroll=4)

    def partial_of(q):
        end = jnp.maximum(plan[1, q] - 1, 0)
        return (sums[end] * jnp.minimum(plan[2, q], 1).astype(jnp.float32)).astype(jnp.bfloat16)

    hops_y = (2, 1, 3, 0)
    sends = {}
    for jy in hops_y:
        yq = (yh + jy) % NY
        for jx in (2, 1, 3):
            outbox[jy, jx] = partial_of(yq * NX + (x + jx) % NX)
            sends[jy, jx] = push(
                outbox.at[jy, jx], inbox_x.at[jy, jx - 1], send_px.at[jy, jx - 1], recv_px.at[jy, jx - 1], {"rep": x_peer(jx)}
            )
        outbox[jy, 0] = partial_of(yq * NX + x)
    total = None
    second = {}
    for jy in hops_y:
        total = outbox[jy, 0].astype(jnp.float32)
        for jx in (1, 3, 2):
            sends[jy, jx].wait_recv()
            total = total + inbox_x[jy, jx - 1].astype(jnp.float32)
        if jy:
            relay_y[jy - 1] = total.astype(jnp.bfloat16)
            second[jy] = push(
                relay_y.at[jy - 1], inbox_y.at[jy - 1], send_py.at[jy - 1], recv_py.at[jy - 1], {"rep": y_peer(jy)}
            )
    for jy in (1, 3, 2):
        second[jy].wait_recv()
        total = total + inbox_y[jy - 1].astype(jnp.float32)
    high = total.astype(jnp.bfloat16)
    low = (total - high.astype(jnp.float32)).astype(jnp.bfloat16)
    hidden = jnp.dot(high, weight[...], preferred_element_type=jnp.float32)
    hidden = hidden + jnp.dot(low, weight[...], preferred_element_type=jnp.float32)
    out_ref[...] = jnp.maximum(hidden + bias[...], 0.0).astype(jnp.bfloat16)
    for copy in sent:
        copy.wait_send()


def shards(features, adj_tiles, tile_rows, tile_cols, tile_counts, weight, out_bias):
    vmem = pl.BlockSpec(memory_space=pltpu.VMEM)
    anywhere = pl.BlockSpec(memory_space=pl.ANY)
    dma = pltpu.SemaphoreType.DMA
    bf16 = jnp.bfloat16
    return pl.pallas_call(
        kernel,
        out_shape=jax.ShapeDtypeStruct((128, 256), bf16),
        in_specs=[anywhere] * 7,
        out_specs=vmem,
        scratch_shapes=[
            pltpu.VMEM((1, 128), jnp.int32),
            pltpu.VMEM((1, 128), jnp.int32),
            pltpu.VMEM((1, 1), jnp.int32),
            pltpu.VMEM((128, 256), bf16),
            pltpu.VMEM((1, 256), jnp.float32),
            pltpu.VMEM((NZ * 2 * 4, HALF, 128), bf16),
            pltpu.VMEM((128, 128, 128), bf16),
            pltpu.VMEM((128, 128, 128), jnp.float32),
            pltpu.VMEM((8, 128), jnp.int32),
            pltpu.SMEM((8, 128), jnp.int32),
            pltpu.VMEM((NY, NX, 128, 128), bf16),
            pltpu.VMEM((NY, NX - 1, 128, 128), bf16),
            pltpu.VMEM((NY - 1, 128, 128), bf16),
            pltpu.VMEM((NY - 1, 128, 128), bf16),
            dma((8,)),
            dma((2, RELAYS + 1, 2)),
            dma((2, RELAYS + 1, 2)),
            dma((NZ + 1,)),
            dma((NZ + 1,)),
            dma((NZ, 3)),
            dma((NZ, 3)),
            dma((NY, NX - 1)),
            dma((NY, NX - 1)),
            dma((NY - 1,)),
            dma((NY - 1,)),
        ],
        compiler_params=pltpu.CompilerParams(
            collective_id=0, has_side_effects=True, vmem_limit_bytes=60 * 1024 * 1024
        ),
        cost_estimate=pl.CostEstimate(flops=2 * 128**4, bytes_accessed=128**3 * 2, transcendentals=0),
        name="layer",
    )(features.reshape(2, HALF, 128), adj_tiles, tile_rows.reshape(1, 128), tile_cols.reshape(1, 128), tile_counts.reshape(1, 1), weight, out_bias.reshape(1, 256))


def solution(mesh):
    in_specs = (
        P(("rep", "section"), None),
        P(("rep", "section"), None, None),
        P(("rep", "section")),
        P(("rep", "section")),
        P(("rep", "section")),
        P(),
        P(),
    )
    out_specs = P(("rep", "section"), None)
    return jax.shard_map(shards, mesh=mesh, in_specs=in_specs, out_specs=out_specs, check_vma=False)
```

```python
import jax
import jax.numpy as jnp
from jax import lax
from jax.experimental import pallas as pl
from jax.experimental.pallas import tpu as pltpu
from jax.sharding import PartitionSpec as P

MESH = pl.DeviceIdType.MESH
NX, NY, NZ = 4, 4, 8
PAIRS = 72


def kernel(
    features, adjacency, rows_in, cols_in, count_in, weight_in, bias_in, out_ref,
    rows_ref, cols_ref, count_ref, weight, bias,
    slab, tiles, sums, plan_v, plan, outbox, inbox_x, relay_y, inbox_y,
    local_sem, send_z, recv_z, send_y, recv_y, send_c, recv_c, send_px, recv_px, send_py, recv_py,
):
    rep, section = lax.axis_index("rep"), lax.axis_index("section")
    yh, x = rep // NX, rep % NX
    y, z, core = section // (2 * NZ), (section // 2) % NZ, section % 2
    partner = (1 - y) * 2 * NZ + z * 2 + core
    sibling = section + 1 - 2 * core

    def at_z(step):
        return y * 2 * NZ + ((z + step + NZ) % NZ) * 2 + core

    def x_peer(step):
        return yh * NX + (x + step) % NX

    def y_peer(step):
        return ((yh + step) % NY) * NX + x

    def block(owner):
        return slab.at[owner + 1]

    small = [
        pltpu.make_async_copy(source, target, local_sem.at[3 + i])
        for i, (source, target) in enumerate(
            ((rows_in, rows_ref), (cols_in, cols_ref), (count_in, count_ref), (weight_in, weight), (bias_in, bias))
        )
    ]
    tile_copy = pltpu.make_async_copy(adjacency, tiles, local_sem.at[0])
    own_copy = pltpu.make_async_copy(features, block(section), local_sem.at[1])
    own_copy.start()
    for copy in small:
        copy.start()
    tile_copy.start()

    barrier = pltpu.get_barrier_semaphore()
    for peer in [at_z(step) for step in range(1, NZ)] + [partner, sibling]:
        pl.semaphore_signal(barrier, inc=1, device_id={"section": peer}, device_id_type=MESH)
    for step in range(1, NX):
        pl.semaphore_signal(barrier, inc=1, device_id={"rep": x_peer(step)}, device_id_type=MESH)
    for step in range(1, NY):
        pl.semaphore_signal(barrier, inc=1, device_id={"rep": y_peer(step)}, device_id_type=MESH)
    own_copy.wait()
    pl.semaphore_wait(barrier, NZ + 1 + NX - 1 + NY - 1)

    sent = []

    def push(source, target, send, recv, peer):
        copy = pltpu.make_async_remote_copy(
            src_ref=source, dst_ref=target, send_sem=send, recv_sem=recv,
            device_id=peer, device_id_type=MESH,
        )
        copy.start()
        sent.append(copy)
        return copy

    def along_z(step):
        ref = block(section)
        return push(ref, ref, send_z.at[step + 3], recv_z.at[step + 3], {"section": at_z(step)})

    def to_partner(owner, slot):
        return push(block(owner), block(owner), send_y.at[slot], recv_y.at[slot], {"section": partner})

    def to_sibling(owner, slot):
        return push(block(owner), block(owner), send_c.at[slot], recv_c.at[slot], {"section": sibling})

    near = (1, -1, 2, -2, 3, -3, 4)
    along = {step: along_z(step) for step in near}
    across = [(section, to_partner(section, 0))]
    siblings = [to_sibling(section, 0)]

    slab[0] = jnp.zeros((128, 128), jnp.bfloat16)
    for copy in small:
        copy.wait()
    lane = lax.broadcasted_iota(jnp.int32, (128, 128), 1)
    down = lax.broadcasted_iota(jnp.int32, (128, 128), 0)
    row_across = jnp.broadcast_to(rows_ref[...], (128, 128))
    row_across = jnp.where(lane < jnp.broadcast_to(count_ref[...], (128, 128)), row_across, NX * NY)
    row_down = row_across.T
    same = row_down == row_across
    earlier = jnp.sum((same & (down < lane)).astype(jnp.int32), axis=0, keepdims=True)
    count = jnp.sum(same.astype(jnp.int32), axis=0, keepdims=True)
    places = 1 + jnp.where(earlier == count - 1, count & 1, 0)
    places_down = jnp.broadcast_to(places, (128, 128)).T
    place = jnp.sum(jnp.where(row_down < row_across, places_down, 0), axis=0, keepdims=True) + earlier
    place_down = jnp.broadcast_to(place, (128, 128)).T
    col_across = jnp.broadcast_to(cols_ref[...], (128, 128))
    info_down = (lane + (col_across + 1) * 128 + row_across * 8192).T
    first = jnp.sum(jnp.where(place_down == 2 * lane, info_down, 0), axis=0, keepdims=True)
    second = jnp.sum(jnp.where(place_down == 2 * lane + 1, info_down, 0), axis=0, keepdims=True)
    ends = jnp.sum(jnp.where(row_down <= lane, places_down, 0), axis=0, keepdims=True)
    used = jnp.sum((row_down == lane).astype(jnp.int32), axis=0, keepdims=True)
    line = lax.broadcasted_iota(jnp.int32, (8, 128), 0)
    plan_v[...] = jnp.where(line == 0, first, jnp.where(line == 1, second, jnp.where(line == 2, ends, used)))
    plan_copy = pltpu.make_async_copy(plan_v, plan, local_sem.at[2])
    plan_copy.start()

    for slot, step in enumerate(near):
        along[step].wait_recv()
        owner = at_z(-step)
        across.append((owner, to_partner(owner, slot + 1)))
        siblings.append(to_sibling(owner, slot + 1))
    for slot, (owner, copy) in enumerate(across):
        copy.wait_recv()
        siblings.append(to_sibling((owner + 2 * NZ) % (4 * NZ), NZ + slot))
    plan_copy.wait()
    tile_copy.wait()
    for copy in siblings:
        copy.wait_recv()

    def step_of(k, carry):
        total, row_before = carry
        one, two = plan[0, k], plan[1, k]
        row = one >> 13
        pair = jnp.concatenate([tiles[one & 127], tiles[two & 127]], axis=1)
        source = jnp.concatenate([slab[(one >> 7) & 63], slab[(two >> 7) & 63]], axis=0)
        product = jnp.dot(pair, source, preferred_element_type=jnp.float32)
        total = total * jnp.where(row == row_before, 1.0, 0.0) + product
        sums[k] = total
        return total, row

    lax.fori_loop(0, PAIRS, step_of, (jnp.zeros((128, 128), jnp.float32), jnp.int32(-1)), unroll=24)

    def partial_of(q):
        end = jnp.maximum((plan[2, q] >> 1) - 1, 0)
        return (sums[end] * jnp.minimum(plan[3, q], 1).astype(jnp.float32)).astype(jnp.bfloat16)

    hops_y = (2, 1, 3, 0)
    sends = {}
    for jy in hops_y:
        yq = (yh + jy) % NY
        for jx in (2, 1, 3):
            outbox[jy, jx] = partial_of(yq * NX + (x + jx) % NX)
            sends[jy, jx] = push(
                outbox.at[jy, jx], inbox_x.at[jy, jx - 1], send_px.at[jy, jx - 1], recv_px.at[jy, jx - 1], {"rep": x_peer(jx)}
            )
        outbox[jy, 0] = partial_of(yq * NX + x)
    total = None
    onward = {}
    for jy in hops_y:
        total = outbox[jy, 0].astype(jnp.float32)
        for jx in (1, 3, 2):
            sends[jy, jx].wait_recv()
            total = total + inbox_x[jy, jx - 1].astype(jnp.float32)
        if jy:
            relay_y[jy - 1] = total.astype(jnp.bfloat16)
            onward[jy] = push(
                relay_y.at[jy - 1], inbox_y.at[jy - 1], send_py.at[jy - 1], recv_py.at[jy - 1], {"rep": y_peer(jy)}
            )
    for jy in (1, 3, 2):
        onward[jy].wait_recv()
        total = total + inbox_y[jy - 1].astype(jnp.float32)
    high = total.astype(jnp.bfloat16)
    low = (total - high.astype(jnp.float32)).astype(jnp.bfloat16)
    hidden = jnp.dot(high, weight[...], preferred_element_type=jnp.float32)
    hidden = hidden + jnp.dot(low, weight[...], preferred_element_type=jnp.float32)
    out_ref[...] = jnp.maximum(hidden + bias[...], 0.0).astype(jnp.bfloat16)
    for copy in sent:
        copy.wait_send()


def shards(features, adj_tiles, tile_rows, tile_cols, tile_counts, weight, out_bias):
    vmem = pl.BlockSpec(memory_space=pltpu.VMEM)
    anywhere = pl.BlockSpec(memory_space=pl.ANY)
    dma = pltpu.SemaphoreType.DMA
    bf16 = jnp.bfloat16
    return pl.pallas_call(
        kernel,
        out_shape=jax.ShapeDtypeStruct((128, 256), bf16),
        in_specs=[anywhere] * 7,
        out_specs=vmem,
        scratch_shapes=[
            pltpu.VMEM((1, 128), jnp.int32),
            pltpu.VMEM((1, 128), jnp.int32),
            pltpu.VMEM((1, 1), jnp.int32),
            pltpu.VMEM((128, 256), bf16),
            pltpu.VMEM((1, 256), jnp.float32),
            pltpu.VMEM((4 * NZ + 1, 128, 128), bf16),
            pltpu.VMEM((128, 128, 128), bf16),
            pltpu.VMEM((PAIRS, 128, 128), jnp.float32),
            pltpu.VMEM((8, 128), jnp.int32),
            pltpu.SMEM((8, 128), jnp.int32),
            pltpu.VMEM((NY, NX, 128, 128), bf16),
            pltpu.VMEM((NY, NX - 1, 128, 128), bf16),
            pltpu.VMEM((NY - 1, 128, 128), bf16),
            pltpu.VMEM((NY - 1, 128, 128), bf16),
            dma((8,)),
            dma((NZ,)),
            dma((NZ,)),
            dma((NZ,)),
            dma((NZ,)),
            dma((2 * NZ,)),
            dma((2 * NZ,)),
            dma((NY, NX - 1)),
            dma((NY, NX - 1)),
            dma((NY - 1,)),
            dma((NY - 1,)),
        ],
        compiler_params=pltpu.CompilerParams(
            collective_id=0, has_side_effects=True, vmem_limit_bytes=60 * 1024 * 1024
        ),
        cost_estimate=pl.CostEstimate(flops=2 * 128**4, bytes_accessed=128**3 * 2, transcendentals=0),
        name="layer",
    )(features, adj_tiles, tile_rows.reshape(1, 128), tile_cols.reshape(1, 128), tile_counts.reshape(1, 1), weight, out_bias.reshape(1, 256))


def solution(mesh):
    in_specs = (
        P(("rep", "section"), None),
        P(("rep", "section"), None, None),
        P(("rep", "section")),
        P(("rep", "section")),
        P(("rep", "section")),
        P(),
        P(),
    )
    out_specs = P(("rep", "section"), None)
    return jax.shard_map(shards, mesh=mesh, in_specs=in_specs, out_specs=out_specs, check_vma=False)
```

```python
import jax
import jax.numpy as jnp
from jax import lax
from jax.experimental import pallas as pl
from jax.experimental.pallas import tpu as pltpu
from jax.sharding import PartitionSpec as P

MESH = pl.DeviceIdType.MESH
NX, NY, NZ = 4, 4, 8
X_FIRST = 96
PAIRS = 72


def kernel(
    features, adjacency, rows_in, cols_in, count_in, weight_in, bias_in, out_ref,
    rows_ref, cols_ref, count_ref, weight, bias,
    slab, tiles, sums, plan_v, plan, outbox, inbox_x, relay_y, inbox_y, inbox_q, relay_x, inbox_r,
    local_sem, send_z, recv_z, send_y, recv_y, send_c, recv_c, send_px, recv_px, send_py, recv_py,
    send_pq, recv_pq, send_pr, recv_pr,
):
    rep, section = lax.axis_index("rep"), lax.axis_index("section")
    yh, x = rep // NX, rep % NX
    y, z, core = section // (2 * NZ), (section // 2) % NZ, section % 2
    partner = (1 - y) * 2 * NZ + z * 2 + core
    sibling = section + 1 - 2 * core

    def at_z(step):
        return y * 2 * NZ + ((z + step + NZ) % NZ) * 2 + core

    def x_peer(step):
        return yh * NX + (x + step) % NX

    def y_peer(step):
        return ((yh + step) % NY) * NX + x

    def block(owner):
        return slab.at[owner + 1]

    small = [
        pltpu.make_async_copy(source, target, local_sem.at[3 + i])
        for i, (source, target) in enumerate(
            ((rows_in, rows_ref), (cols_in, cols_ref), (count_in, count_ref), (weight_in, weight), (bias_in, bias))
        )
    ]
    tile_copy = pltpu.make_async_copy(adjacency, tiles, local_sem.at[0])
    own_copy = pltpu.make_async_copy(features, block(section), local_sem.at[1])
    own_copy.start()
    for copy in small:
        copy.start()
    tile_copy.start()

    barrier = pltpu.get_barrier_semaphore()
    for peer in [at_z(step) for step in range(1, NZ)] + [partner, sibling]:
        pl.semaphore_signal(barrier, inc=1, device_id={"section": peer}, device_id_type=MESH)
    for step in range(1, NX):
        pl.semaphore_signal(barrier, inc=1, device_id={"rep": x_peer(step)}, device_id_type=MESH)
    for step in range(1, NY):
        pl.semaphore_signal(barrier, inc=1, device_id={"rep": y_peer(step)}, device_id_type=MESH)
    own_copy.wait()
    pl.semaphore_wait(barrier, NZ + 1 + NX - 1 + NY - 1)

    sent = []

    def push(source, target, send, recv, peer):
        copy = pltpu.make_async_remote_copy(
            src_ref=source, dst_ref=target, send_sem=send, recv_sem=recv,
            device_id=peer, device_id_type=MESH,
        )
        copy.start()
        sent.append(copy)
        return copy

    def along_z(step):
        ref = block(section)
        return push(ref, ref, send_z.at[step + 3], recv_z.at[step + 3], {"section": at_z(step)})

    def to_partner(owner, slot):
        return push(block(owner), block(owner), send_y.at[slot], recv_y.at[slot], {"section": partner})

    def to_sibling(owner, slot):
        return push(block(owner), block(owner), send_c.at[slot], recv_c.at[slot], {"section": sibling})

    near = (1, -1, 2, -2, 3, -3, 4)
    along = {step: along_z(step) for step in near}
    across = [(section, to_partner(section, 0))]
    siblings = [to_sibling(section, 0)]

    slab[0] = jnp.zeros((128, 128), jnp.bfloat16)
    for copy in small:
        copy.wait()
    lane = lax.broadcasted_iota(jnp.int32, (128, 128), 1)
    down = lax.broadcasted_iota(jnp.int32, (128, 128), 0)
    row_across = jnp.broadcast_to(rows_ref[...], (128, 128))
    row_across = jnp.where(lane < jnp.broadcast_to(count_ref[...], (128, 128)), row_across, NX * NY)
    row_down = row_across.T
    same = row_down == row_across
    earlier = jnp.sum((same & (down < lane)).astype(jnp.int32), axis=0, keepdims=True)
    count = jnp.sum(same.astype(jnp.int32), axis=0, keepdims=True)
    places = 1 + jnp.where(earlier == count - 1, count & 1, 0)
    places_down = jnp.broadcast_to(places, (128, 128)).T
    place = jnp.sum(jnp.where(row_down < row_across, places_down, 0), axis=0, keepdims=True) + earlier
    place_down = jnp.broadcast_to(place, (128, 128)).T
    col_across = jnp.broadcast_to(cols_ref[...], (128, 128))
    info_down = (lane + (col_across + 1) * 128 + row_across * 8192).T
    first = jnp.sum(jnp.where(place_down == 2 * lane, info_down, 0), axis=0, keepdims=True)
    second = jnp.sum(jnp.where(place_down == 2 * lane + 1, info_down, 0), axis=0, keepdims=True)
    ends = jnp.sum(jnp.where(row_down <= lane, places_down, 0), axis=0, keepdims=True)
    used = jnp.sum((row_down == lane).astype(jnp.int32), axis=0, keepdims=True)
    line = lax.broadcasted_iota(jnp.int32, (8, 128), 0)
    plan_v[...] = jnp.where(line == 0, first, jnp.where(line == 1, second, jnp.where(line == 2, ends, used)))
    plan_copy = pltpu.make_async_copy(plan_v, plan, local_sem.at[2])
    plan_copy.start()

    for slot, step in enumerate(near):
        along[step].wait_recv()
        owner = at_z(-step)
        across.append((owner, to_partner(owner, slot + 1)))
        siblings.append(to_sibling(owner, slot + 1))
    for slot, (owner, copy) in enumerate(across):
        copy.wait_recv()
        siblings.append(to_sibling((owner + 2 * NZ) % (4 * NZ), NZ + slot))
    plan_copy.wait()
    tile_copy.wait()
    for copy in siblings:
        copy.wait_recv()

    def step_of(k, carry):
        total, row_before = carry
        one, two = plan[0, k], plan[1, k]
        row = one >> 13
        pair = jnp.concatenate([tiles[one & 127], tiles[two & 127]], axis=1)
        source = jnp.concatenate([slab[(one >> 7) & 63], slab[(two >> 7) & 63]], axis=0)
        product = jnp.dot(pair, source, preferred_element_type=jnp.float32)
        total = total * jnp.where(row == row_before, 1.0, 0.0) + product
        sums[k] = total
        return total, row

    lax.fori_loop(0, PAIRS, step_of, (jnp.zeros((128, 128), jnp.float32), jnp.int32(-1)), unroll=24)

    def partial_of(q):
        end = jnp.maximum((plan[2, q] >> 1) - 1, 0)
        return (sums[end] * jnp.minimum(plan[3, q], 1).astype(jnp.float32)).astype(jnp.bfloat16)

    for jy in range(NY):
        for jx in range(NX):
            outbox[jy, jx] = partial_of(((yh + jy) % NY) * NX + (x + jx) % NX)
    upper, lower = pl.ds(0, X_FIRST), pl.ds(X_FIRST, 128 - X_FIRST)
    hops = (2, 1, 3, 0)
    by_x, by_y = {}, {}
    for j in hops:
        for step in hops[:3]:
            by_x[j, step] = push(
                outbox.at[j, step, upper], inbox_x.at[j, step - 1],
                send_px.at[j, step - 1], recv_px.at[j, step - 1], {"rep": x_peer(step)},
            )
        for step in hops[:3]:
            by_y[j, step] = push(
                outbox.at[step, j, lower], inbox_q.at[j, step - 1],
                send_pq.at[j, step - 1], recv_pq.at[j, step - 1], {"rep": y_peer(step)},
            )
    then_y, then_x = {}, {}
    for j in hops:
        total = outbox[j, 0, upper].astype(jnp.float32)
        for step in (1, 3, 2):
            by_x[j, step].wait_recv()
            total = total + inbox_x[j, step - 1].astype(jnp.float32)
        if j:
            relay_y[j - 1] = total.astype(jnp.bfloat16)
            then_y[j] = push(
                relay_y.at[j - 1], inbox_y.at[j - 1], send_py.at[j - 1], recv_py.at[j - 1], {"rep": y_peer(j)}
            )
        under = outbox[0, j, lower].astype(jnp.float32)
        for step in (1, 3, 2):
            by_y[j, step].wait_recv()
            under = under + inbox_q[j, step - 1].astype(jnp.float32)
        if j:
            relay_x[j - 1] = under.astype(jnp.bfloat16)
            then_x[j] = push(
                relay_x.at[j - 1], inbox_r.at[j - 1], send_pr.at[j - 1], recv_pr.at[j - 1], {"rep": x_peer(j)}
            )
    for j in (1, 3, 2):
        then_x[j].wait_recv()
        under = under + inbox_r[j - 1].astype(jnp.float32)
    for j in (1, 3, 2):
        then_y[j].wait_recv()
        total = total + inbox_y[j - 1].astype(jnp.float32)
    total = jnp.concatenate([total, under], axis=0)
    high = total.astype(jnp.bfloat16)
    low = (total - high.astype(jnp.float32)).astype(jnp.bfloat16)
    hidden = jnp.dot(high, weight[...], preferred_element_type=jnp.float32)
    hidden = hidden + jnp.dot(low, weight[...], preferred_element_type=jnp.float32)
    out_ref[...] = jnp.maximum(hidden + bias[...], 0.0).astype(jnp.bfloat16)
    for copy in sent:
        copy.wait_send()


def shards(features, adj_tiles, tile_rows, tile_cols, tile_counts, weight, out_bias):
    vmem = pl.BlockSpec(memory_space=pltpu.VMEM)
    anywhere = pl.BlockSpec(memory_space=pl.ANY)
    dma = pltpu.SemaphoreType.DMA
    bf16 = jnp.bfloat16
    return pl.pallas_call(
        kernel,
        out_shape=jax.ShapeDtypeStruct((128, 256), bf16),
        in_specs=[anywhere] * 7,
        out_specs=vmem,
        scratch_shapes=[
            pltpu.VMEM((1, 128), jnp.int32),
            pltpu.VMEM((1, 128), jnp.int32),
            pltpu.VMEM((1, 1), jnp.int32),
            pltpu.VMEM((128, 256), bf16),
            pltpu.VMEM((1, 256), jnp.float32),
            pltpu.VMEM((4 * NZ + 1, 128, 128), bf16),
            pltpu.VMEM((128, 128, 128), bf16),
            pltpu.VMEM((PAIRS, 128, 128), jnp.float32),
            pltpu.VMEM((8, 128), jnp.int32),
            pltpu.SMEM((8, 128), jnp.int32),
            pltpu.VMEM((NY, NX, 128, 128), bf16),
            pltpu.VMEM((NY, NX - 1, X_FIRST, 128), bf16),
            pltpu.VMEM((NY - 1, X_FIRST, 128), bf16),
            pltpu.VMEM((NY - 1, X_FIRST, 128), bf16),
            pltpu.VMEM((NX, NY - 1, 128 - X_FIRST, 128), bf16),
            pltpu.VMEM((NX - 1, 128 - X_FIRST, 128), bf16),
            pltpu.VMEM((NX - 1, 128 - X_FIRST, 128), bf16),
            dma((8,)),
            dma((NZ,)),
            dma((NZ,)),
            dma((NZ,)),
            dma((NZ,)),
            dma((2 * NZ,)),
            dma((2 * NZ,)),
            dma((NY, NX - 1)),
            dma((NY, NX - 1)),
            dma((NY - 1,)),
            dma((NY - 1,)),
            dma((NX, NY - 1)),
            dma((NX, NY - 1)),
            dma((NX - 1,)),
            dma((NX - 1,)),
        ],
        compiler_params=pltpu.CompilerParams(
            collective_id=0, has_side_effects=True, vmem_limit_bytes=60 * 1024 * 1024
        ),
        cost_estimate=pl.CostEstimate(flops=2 * 128**4, bytes_accessed=128**3 * 2, transcendentals=0),
        name="layer",
    )(features, adj_tiles, tile_rows.reshape(1, 128), tile_cols.reshape(1, 128), tile_counts.reshape(1, 1), weight, out_bias.reshape(1, 256))


def solution(mesh):
    in_specs = (
        P(("rep", "section"), None),
        P(("rep", "section"), None, None),
        P(("rep", "section")),
        P(("rep", "section")),
        P(("rep", "section")),
        P(),
        P(),
    )
    out_specs = P(("rep", "section"), None)
    return jax.shard_map(shards, mesh=mesh, in_specs=in_specs, out_specs=out_specs, check_vma=False)
```

```python
import jax
import jax.numpy as jnp
from jax import lax
from jax.experimental import pallas as pl
from jax.experimental.pallas import tpu as pltpu
from jax.sharding import PartitionSpec as P

MESH = pl.DeviceIdType.MESH
NX, NY, NZ = 4, 4, 8
X_FIRST = 80
PAIRS = 72


def kernel(
    features, adjacency, rows_in, cols_in, count_in, out_ref,
    rows_ref, cols_ref, count_ref,
    slab, tiles, sums, plan_v, plan, outbox, inbox_x, relay_y, inbox_y, inbox_q, relay_x, inbox_r,
    local_sem, send_z, recv_z, send_y, recv_y, send_c, recv_c, send_px, recv_px, send_py, recv_py,
    send_pq, recv_pq, send_pr, recv_pr,
):
    rep, section = lax.axis_index("rep"), lax.axis_index("section")
    yh, x = rep // NX, rep % NX
    y, z, core = section // (2 * NZ), (section // 2) % NZ, section % 2
    partner = (1 - y) * 2 * NZ + z * 2 + core
    sibling = section + 1 - 2 * core

    def at_z(step):
        return y * 2 * NZ + ((z + step + NZ) % NZ) * 2 + core

    def x_peer(step):
        return yh * NX + (x + step) % NX

    def y_peer(step):
        return ((yh + step) % NY) * NX + x

    def block(owner):
        return slab.at[owner + 1]

    barrier = pltpu.get_barrier_semaphore()
    for peer in [at_z(step) for step in (4, 3, 5, 2, 6, 1, 7)] + [partner, sibling]:
        pl.semaphore_signal(barrier, inc=1, device_id={"section": peer}, device_id_type=MESH)
    for step in range(1, NX):
        pl.semaphore_signal(barrier, inc=1, device_id={"rep": x_peer(step)}, device_id_type=MESH)
    for step in range(1, NY):
        pl.semaphore_signal(barrier, inc=1, device_id={"rep": y_peer(step)}, device_id_type=MESH)
    small = [
        pltpu.make_async_copy(source, target, local_sem.at[3 + i])
        for i, (source, target) in enumerate(
            ((rows_in, rows_ref), (cols_in, cols_ref), (count_in, count_ref))
        )
    ]
    tile_copy = pltpu.make_async_copy(adjacency, tiles, local_sem.at[0])
    own_copy = pltpu.make_async_copy(features, block(section), local_sem.at[1])
    own_copy.start()
    for copy in small:
        copy.start()
    tile_copy.start()

    own_copy.wait()
    pl.semaphore_wait(barrier, NZ + 1 + NX - 1 + NY - 1)

    sent = [[]]

    def push(source, target, send, recv, peer):
        copy = pltpu.make_async_remote_copy(
            src_ref=source, dst_ref=target, send_sem=send, recv_sem=recv,
            device_id=peer, device_id_type=MESH,
        )
        copy.start()
        sent[-1].append(copy)
        return copy

    def along_z(step):
        ref = block(section)
        return push(ref, ref, send_z.at[step + 3], recv_z.at[step + 3], {"section": at_z(step)})

    def to_partner(owner, slot):
        return push(block(owner), block(owner), send_y.at[slot], recv_y.at[slot], {"section": partner})

    def to_sibling(owner, slot):
        return push(block(owner), block(owner), send_c.at[slot], recv_c.at[slot], {"section": sibling})

    near = (1, -1, 2, -2, 3, -3, 4)
    along = {step: along_z(step) for step in near}
    across = [(section, to_partner(section, 0))]
    siblings = [to_sibling(section, 0)]

    slab[0] = jnp.zeros((128, 128), jnp.bfloat16)
    for copy in small:
        copy.wait()
    lane = lax.broadcasted_iota(jnp.int32, (128, 128), 1)
    down = lax.broadcasted_iota(jnp.int32, (128, 128), 0)
    row_across = jnp.broadcast_to(rows_ref[...], (128, 128))
    row_across = jnp.where(lane < jnp.broadcast_to(count_ref[...], (128, 128)), row_across, NX * NY)
    row_down = row_across.T
    same = row_down == row_across
    earlier = jnp.sum((same & (down < lane)).astype(jnp.int32), axis=0, keepdims=True)
    count = jnp.sum(same.astype(jnp.int32), axis=0, keepdims=True)
    places = 1 + jnp.where(earlier == count - 1, count & 1, 0)
    places_down = jnp.broadcast_to(places, (128, 128)).T
    place = jnp.sum(jnp.where(row_down < row_across, places_down, 0), axis=0, keepdims=True) + earlier
    place_down = jnp.broadcast_to(place, (128, 128)).T
    col_across = jnp.broadcast_to(cols_ref[...], (128, 128))
    info_down = (lane + (col_across + 1) * 128 + row_across * 8192).T
    first = jnp.sum(jnp.where(place_down == 2 * lane, info_down, 0), axis=0, keepdims=True)
    second = jnp.sum(jnp.where(place_down == 2 * lane + 1, info_down, 0), axis=0, keepdims=True)
    ends = jnp.sum(jnp.where(row_down <= lane, places_down, 0), axis=0, keepdims=True)
    used = jnp.sum((row_down == lane).astype(jnp.int32), axis=0, keepdims=True)
    line = lax.broadcasted_iota(jnp.int32, (8, 128), 0)
    plan_v[...] = jnp.where(line == 0, first, jnp.where(line == 1, second, jnp.where(line == 2, ends, used)))
    plan_copy = pltpu.make_async_copy(plan_v, plan, local_sem.at[2])
    plan_copy.start()

    for slot, step in enumerate(near):
        along[step].wait_recv()
        owner = at_z(-step)
        across.append((owner, to_partner(owner, slot + 1)))
        siblings.append(to_sibling(owner, slot + 1))
    for slot, (owner, copy) in enumerate(across):
        copy.wait_recv()
        siblings.append(to_sibling((owner + 2 * NZ) % (4 * NZ), NZ + slot))
    plan_copy.wait()
    tile_copy.wait()
    for copy in siblings:
        copy.wait_recv()

    def step_of(k, carry):
        total, row_before = carry
        one, two = plan[0, k], plan[1, k]
        row = one >> 13
        pair = jnp.concatenate([tiles[one & 127], tiles[two & 127]], axis=1)
        source = jnp.concatenate([slab[(one >> 7) & 63], slab[(two >> 7) & 63]], axis=0)
        product = jnp.dot(pair, source, preferred_element_type=jnp.float32)
        total = total * jnp.where(row == row_before, 1.0, 0.0) + product
        sums[k] = total
        return total, row

    lax.fori_loop(0, PAIRS, step_of, (jnp.zeros((128, 128), jnp.float32), jnp.int32(-1)), unroll=36)

    def partial_of(q):
        end = jnp.maximum((plan[2, q] >> 1) - 1, 0)
        return (sums[end] * jnp.minimum(plan[3, q], 1).astype(jnp.float32)).astype(jnp.bfloat16)

    for jy in range(NY):
        for jx in range(NX):
            outbox[jy, jx] = partial_of(((yh + jy) % NY) * NX + (x + jx) % NX)
    upper, lower = pl.ds(0, X_FIRST), pl.ds(X_FIRST, 128 - X_FIRST)
    hops = (2, 1, 3, 0)
    gathered = sent[0]
    sent.append([])
    by_x, by_y = {}, {}
    for j in hops:
        for step in hops[:3]:
            by_x[j, step] = push(
                outbox.at[j, step, upper], inbox_x.at[j, step - 1],
                send_px.at[j, step - 1], recv_px.at[j, step - 1], {"rep": x_peer(step)},
            )
        for step in hops[:3]:
            by_y[j, step] = push(
                outbox.at[step, j, lower], inbox_q.at[j, step - 1],
                send_pq.at[j, step - 1], recv_pq.at[j, step - 1], {"rep": y_peer(step)},
            )
    for copy in gathered:
        copy.wait_send()
    then_y, then_x = {}, {}
    for j in hops:
        total = outbox[j, 0, upper].astype(jnp.float32)
        for step in (1, 3, 2):
            by_x[j, step].wait_recv()
            total = total + inbox_x[j, step - 1].astype(jnp.float32)
        if j:
            relay_y[j - 1] = total.astype(jnp.bfloat16)
            then_y[j] = push(
                relay_y.at[j - 1], inbox_y.at[j - 1], send_py.at[j - 1], recv_py.at[j - 1], {"rep": y_peer(j)}
            )
        under = outbox[0, j, lower].astype(jnp.float32)
        for step in (1, 3, 2):
            by_y[j, step].wait_recv()
            under = under + inbox_q[j, step - 1].astype(jnp.float32)
        if j:
            relay_x[j - 1] = under.astype(jnp.bfloat16)
            then_x[j] = push(
                relay_x.at[j - 1], inbox_r.at[j - 1], send_pr.at[j - 1], recv_pr.at[j - 1], {"rep": x_peer(j)}
            )
    for j in (1, 3, 2):
        then_x[j].wait_recv()
        under = under + inbox_r[j - 1].astype(jnp.float32)
    for j in (1, 3, 2):
        then_y[j].wait_recv()
        total = total + inbox_y[j - 1].astype(jnp.float32)
    total = jnp.concatenate([total, under], axis=0)
    out_ref[...] = total.astype(jnp.bfloat16)
    for copy in sent[1]:
        copy.wait_send()


def shards(features, adj_tiles, tile_rows, tile_cols, tile_counts, weight, out_bias):
    vmem = pl.BlockSpec(memory_space=pltpu.VMEM)
    anywhere = pl.BlockSpec(memory_space=pl.ANY)
    dma = pltpu.SemaphoreType.DMA
    bf16 = jnp.bfloat16
    summed = pl.pallas_call(
        kernel,
        out_shape=jax.ShapeDtypeStruct((128, 128), bf16),
        in_specs=[anywhere] * 5,
        out_specs=vmem,
        scratch_shapes=[
            pltpu.VMEM((1, 128), jnp.int32),
            pltpu.VMEM((1, 128), jnp.int32),
            pltpu.VMEM((1, 1), jnp.int32),
            pltpu.VMEM((4 * NZ + 1, 128, 128), bf16),
            pltpu.VMEM((128, 128, 128), bf16),
            pltpu.VMEM((PAIRS, 128, 128), jnp.float32),
            pltpu.VMEM((8, 128), jnp.int32),
            pltpu.SMEM((8, 128), jnp.int32),
            pltpu.VMEM((NY, NX, 128, 128), bf16),
            pltpu.VMEM((NY, NX - 1, X_FIRST, 128), bf16),
            pltpu.VMEM((NY - 1, X_FIRST, 128), bf16),
            pltpu.VMEM((NY - 1, X_FIRST, 128), bf16),
            pltpu.VMEM((NX, NY - 1, 128 - X_FIRST, 128), bf16),
            pltpu.VMEM((NX - 1, 128 - X_FIRST, 128), bf16),
            pltpu.VMEM((NX - 1, 128 - X_FIRST, 128), bf16),
            dma((8,)),
            dma((NZ,)),
            dma((NZ,)),
            dma((NZ,)),
            dma((NZ,)),
            dma((2 * NZ,)),
            dma((2 * NZ,)),
            dma((NY, NX - 1)),
            dma((NY, NX - 1)),
            dma((NY - 1,)),
            dma((NY - 1,)),
            dma((NX, NY - 1)),
            dma((NX, NY - 1)),
            dma((NX - 1,)),
            dma((NX - 1,)),
        ],
        compiler_params=pltpu.CompilerParams(
            collective_id=0, has_side_effects=True, vmem_limit_bytes=60 * 1024 * 1024
        ),
        cost_estimate=pl.CostEstimate(flops=2 * 128**4, bytes_accessed=128**3 * 2, transcendentals=0),
        name="layer",
    )(features, adj_tiles, tile_rows.reshape(1, 128), tile_cols.reshape(1, 128), tile_counts.reshape(1, 1))
    hidden = jnp.dot(summed, weight, preferred_element_type=jnp.float32)
    return jnp.maximum(hidden + out_bias, 0.0).astype(bf16)


def solution(mesh):
    in_specs = (
        P(("rep", "section"), None),
        P(("rep", "section"), None, None),
        P(("rep", "section")),
        P(("rep", "section")),
        P(("rep", "section")),
        P(),
        P(),
    )
    out_specs = P(("rep", "section"), None)
    return jax.shard_map(shards, mesh=mesh, in_specs=in_specs, out_specs=out_specs, check_vma=False)
```

```python
import jax
import jax.numpy as jnp
from jax import lax
from jax.experimental import pallas as pl
from jax.experimental.pallas import tpu as pltpu
from jax.sharding import PartitionSpec as P

MESH = pl.DeviceIdType.MESH
NX, NY, NZ = 4, 4, 8
X_FIRST = 80
PAIRS = 72


def kernel(
    features, adjacency, rows_in, cols_in, count_in, out_ref,
    rows_ref, cols_ref, count_ref,
    slab, tiles, sums, plan_v, plan, outbox, inbox_x, relay_y, inbox_y, inbox_q, relay_x, inbox_r,
    local_sem, send_z, recv_z, send_y, recv_y, send_c, recv_c, send_px, recv_px, send_py, recv_py,
    send_pq, recv_pq, send_pr, recv_pr,
):
    rep, section = lax.axis_index("rep"), lax.axis_index("section")
    yh, x = rep // NX, rep % NX
    y, z, core = section // (2 * NZ), (section // 2) % NZ, section % 2
    partner = (1 - y) * 2 * NZ + z * 2 + core
    sibling = section + 1 - 2 * core

    def at_z(step):
        return y * 2 * NZ + ((z + step + NZ) % NZ) * 2 + core

    def x_peer(step):
        return yh * NX + (x + step) % NX

    def y_peer(step):
        return ((yh + step) % NY) * NX + x

    def block(owner):
        return slab.at[owner + 1]

    barrier = pltpu.get_barrier_semaphore()
    for peer in [at_z(step) for step in (4, 3, 5, 2, 6, 1, 7)] + [partner, sibling]:
        pl.semaphore_signal(barrier, inc=1, device_id={"section": peer}, device_id_type=MESH)
    for step in range(1, NX):
        pl.semaphore_signal(barrier, inc=1, device_id={"rep": x_peer(step)}, device_id_type=MESH)
    for step in range(1, NY):
        pl.semaphore_signal(barrier, inc=1, device_id={"rep": y_peer(step)}, device_id_type=MESH)
    small = [
        pltpu.make_async_copy(source, target, local_sem.at[3 + i])
        for i, (source, target) in enumerate(
            ((rows_in, rows_ref), (cols_in, cols_ref), (count_in, count_ref))
        )
    ]
    tile_copy = pltpu.make_async_copy(adjacency, tiles, local_sem.at[0])
    own_copy = pltpu.make_async_copy(features, block(section), local_sem.at[1])
    own_copy.start()
    for copy in small:
        copy.start()
    tile_copy.start()

    own_copy.wait()
    pl.semaphore_wait(barrier, NZ + 1 + NX - 1 + NY - 1)

    sent = [[]]

    def push(source, target, send, recv, peer):
        copy = pltpu.make_async_remote_copy(
            src_ref=source, dst_ref=target, send_sem=send, recv_sem=recv,
            device_id=peer, device_id_type=MESH,
        )
        copy.start()
        sent[-1].append(copy)
        return copy

    def along_z(step):
        ref = block(section)
        return push(ref, ref, send_z.at[step + 3], recv_z.at[step + 3], {"section": at_z(step)})

    def to_partner(owner, slot):
        return push(block(owner), block(owner), send_y.at[slot], recv_y.at[slot], {"section": partner})

    def to_sibling(owner, slot):
        return push(block(owner), block(owner), send_c.at[slot], recv_c.at[slot], {"section": sibling})

    near = (1, -1, 2, -2, 3, -3, 4)
    along = {step: along_z(step) for step in near}
    across = [(section, to_partner(section, 0))]
    siblings = [to_sibling(section, 0)]

    slab[0] = jnp.zeros((128, 128), jnp.bfloat16)
    for copy in small:
        copy.wait()
    lane = lax.broadcasted_iota(jnp.int32, (128, 128), 1)
    down = lax.broadcasted_iota(jnp.int32, (128, 128), 0)
    row_across = jnp.broadcast_to(rows_ref[...], (128, 128))
    row_across = jnp.where(lane < jnp.broadcast_to(count_ref[...], (128, 128)), row_across, NX * NY)
    row_down = row_across.T
    same = row_down == row_across
    earlier = jnp.sum((same & (down < lane)).astype(jnp.int32), axis=0, keepdims=True)
    count = jnp.sum(same.astype(jnp.int32), axis=0, keepdims=True)
    places = 1 + jnp.where(earlier == count - 1, count & 1, 0)
    places_down = jnp.broadcast_to(places, (128, 128)).T
    place = jnp.sum(jnp.where(row_down < row_across, places_down, 0), axis=0, keepdims=True) + earlier
    place_down = jnp.broadcast_to(place, (128, 128)).T
    col_across = jnp.broadcast_to(cols_ref[...], (128, 128))
    info_down = (lane + (col_across + 1) * 128 + row_across * 8192).T
    first = jnp.sum(jnp.where(place_down == 2 * lane, info_down, 0), axis=0, keepdims=True)
    second = jnp.sum(jnp.where(place_down == 2 * lane + 1, info_down, 0), axis=0, keepdims=True)
    ends = jnp.sum(jnp.where(row_down <= lane, places_down, 0), axis=0, keepdims=True)
    used = jnp.sum((row_down == lane).astype(jnp.int32), axis=0, keepdims=True)
    line = lax.broadcasted_iota(jnp.int32, (8, 128), 0)
    plan_v[...] = jnp.where(line == 0, first, jnp.where(line == 1, second, jnp.where(line == 2, ends, used)))
    plan_copy = pltpu.make_async_copy(plan_v, plan, local_sem.at[2])
    plan_copy.start()

    for slot, step in enumerate(near):
        along[step].wait_recv()
        owner = at_z(-step)
        across.append((owner, to_partner(owner, slot + 1)))
        siblings.append(to_sibling(owner, slot + 1))
    for slot, (owner, copy) in enumerate(across):
        copy.wait_recv()
        siblings.append(to_sibling((owner + 2 * NZ) % (4 * NZ), NZ + slot))
    plan_copy.wait()
    tile_copy.wait()
    for copy in siblings:
        copy.wait_recv()

    def step_of(k, carry):
        total, row_before = carry
        one, two = plan[0, k], plan[1, k]
        row = one >> 13
        pair = jnp.concatenate([tiles[one & 127], tiles[two & 127]], axis=1)
        source = jnp.concatenate([slab[(one >> 7) & 63], slab[(two >> 7) & 63]], axis=0)
        product = jnp.dot(pair, source, preferred_element_type=jnp.float32)
        total = total * jnp.where(row == row_before, 1.0, 0.0) + product
        sums[k] = total
        return total, row

    lax.fori_loop(0, PAIRS, step_of, (jnp.zeros((128, 128), jnp.float32), jnp.int32(-1)), unroll=36)

    def partial_of(q):
        end = jnp.maximum((plan[2, q] >> 1) - 1, 0)
        return (sums[end] * jnp.minimum(plan[3, q], 1).astype(jnp.float32)).astype(jnp.bfloat16)

    for jy in range(NY):
        for jx in range(NX):
            outbox[jy, jx] = partial_of(((yh + jy) % NY) * NX + (x + jx) % NX)
    upper, lower = pl.ds(0, X_FIRST), pl.ds(X_FIRST, 128 - X_FIRST)
    hops = (2, 1, 3, 0)
    gathered = sent[0]
    sent.append([])
    by_x, by_y = {}, {}
    for j in hops:
        for step in hops[:3]:
            by_x[j, step] = push(
                outbox.at[j, step, upper], inbox_x.at[j, step - 1],
                send_px.at[j, step - 1], recv_px.at[j, step - 1], {"rep": x_peer(step)},
            )
    for j in hops:
        for step in hops[:3]:
            by_y[j, step] = push(
                outbox.at[step, j, lower], inbox_q.at[j, step - 1],
                send_pq.at[j, step - 1], recv_pq.at[j, step - 1], {"rep": y_peer(step)},
            )
    for copy in gathered:
        copy.wait_send()
    then_y, then_x = {}, {}
    for j in hops:
        total = outbox[j, 0, upper].astype(jnp.float32)
        for step in (1, 3, 2):
            by_x[j, step].wait_recv()
            total = total + inbox_x[j, step - 1].astype(jnp.float32)
        if j:
            relay_y[j - 1] = total.astype(jnp.bfloat16)
            then_y[j] = push(
                relay_y.at[j - 1], inbox_y.at[j - 1], send_py.at[j - 1], recv_py.at[j - 1], {"rep": y_peer(j)}
            )
        under = outbox[0, j, lower].astype(jnp.float32)
        for step in (1, 3, 2):
            by_y[j, step].wait_recv()
            under = under + inbox_q[j, step - 1].astype(jnp.float32)
        if j:
            relay_x[j - 1] = under.astype(jnp.bfloat16)
            then_x[j] = push(
                relay_x.at[j - 1], inbox_r.at[j - 1], send_pr.at[j - 1], recv_pr.at[j - 1], {"rep": x_peer(j)}
            )
    for j in (1, 3, 2):
        then_x[j].wait_recv()
        under = under + inbox_r[j - 1].astype(jnp.float32)
    for j in (1, 3, 2):
        then_y[j].wait_recv()
        total = total + inbox_y[j - 1].astype(jnp.float32)
    total = jnp.concatenate([total, under], axis=0)
    out_ref[...] = total.astype(jnp.bfloat16)
    for copy in sent[1]:
        copy.wait_send()


def shards(features, adj_tiles, tile_rows, tile_cols, tile_counts, weight, out_bias):
    vmem = pl.BlockSpec(memory_space=pltpu.VMEM)
    anywhere = pl.BlockSpec(memory_space=pl.ANY)
    dma = pltpu.SemaphoreType.DMA
    bf16 = jnp.bfloat16
    summed = pl.pallas_call(
        kernel,
        out_shape=jax.ShapeDtypeStruct((128, 128), bf16),
        in_specs=[anywhere] * 5,
        out_specs=vmem,
        scratch_shapes=[
            pltpu.VMEM((1, 128), jnp.int32),
            pltpu.VMEM((1, 128), jnp.int32),
            pltpu.VMEM((1, 1), jnp.int32),
            pltpu.VMEM((4 * NZ + 1, 128, 128), bf16),
            pltpu.VMEM((128, 128, 128), bf16),
            pltpu.VMEM((PAIRS, 128, 128), jnp.float32),
            pltpu.VMEM((8, 128), jnp.int32),
            pltpu.SMEM((8, 128), jnp.int32),
            pltpu.VMEM((NY, NX, 128, 128), bf16),
            pltpu.VMEM((NY, NX - 1, X_FIRST, 128), bf16),
            pltpu.VMEM((NY - 1, X_FIRST, 128), bf16),
            pltpu.VMEM((NY - 1, X_FIRST, 128), bf16),
            pltpu.VMEM((NX, NY - 1, 128 - X_FIRST, 128), bf16),
            pltpu.VMEM((NX - 1, 128 - X_FIRST, 128), bf16),
            pltpu.VMEM((NX - 1, 128 - X_FIRST, 128), bf16),
            dma((8,)),
            dma((NZ,)),
            dma((NZ,)),
            dma((NZ,)),
            dma((NZ,)),
            dma((2 * NZ,)),
            dma((2 * NZ,)),
            dma((NY, NX - 1)),
            dma((NY, NX - 1)),
            dma((NY - 1,)),
            dma((NY - 1,)),
            dma((NX, NY - 1)),
            dma((NX, NY - 1)),
            dma((NX - 1,)),
            dma((NX - 1,)),
        ],
        compiler_params=pltpu.CompilerParams(
            collective_id=0, has_side_effects=True, vmem_limit_bytes=60 * 1024 * 1024
        ),
        cost_estimate=pl.CostEstimate(flops=2 * 128**4, bytes_accessed=128**3 * 2, transcendentals=0),
        name="layer",
    )(features, adj_tiles, tile_rows.reshape(1, 128), tile_cols.reshape(1, 128), tile_counts.reshape(1, 1))
    hidden = jnp.dot(summed, weight, preferred_element_type=jnp.float32)
    return jnp.maximum(hidden + out_bias, 0.0).astype(bf16)


def solution(mesh):
    in_specs = (
        P(("rep", "section"), None),
        P(("rep", "section"), None, None),
        P(("rep", "section")),
        P(("rep", "section")),
        P(("rep", "section")),
        P(),
        P(),
    )
    out_specs = P(("rep", "section"), None)
    return jax.shard_map(shards, mesh=mesh, in_specs=in_specs, out_specs=out_specs, check_vma=False)
```
